32 devices in a mesh: batch: 8 (over z, x), tensor: 4 (over y, core).
Axes of the slice: x: 2, y: 2, z: 4, core: 2. Of those that a mesh axis runs over, the one named last changes fastest.
Arguments:
- tokens: bfloat16 [16384, 512], P('batch', 'tensor'), may hold values from -6 to 6
- cotangent: float32 [16384, 512], P('batch', 'tensor'), may hold values from -6 to 6
- query_weight: bfloat16 [512, 512], P(None, 'tensor'), may hold values from -0.25 to 0.25
- key_weight: bfloat16 [512, 512], P(None, 'tensor'), may hold values from -0.25 to 0.25
- value_weight: bfloat16 [512, 512], P(None, 'tensor'), may hold values from -0.25 to 0.25
- output_weight: bfloat16 [512, 512], P('tensor'), may hold values from -0.75 to 0.75
- up_weight: bfloat16 [512, 2048], P(None, 'tensor'), may hold values from -0.25 to 0.25
- down_weight: bfloat16 [2048, 512], P('tensor'), may hold values from -0.125 to 0.125
- first_gate: bfloat16 [512, 512], P(None, 'tensor'), may hold values from -0.25 to 0.25
- second_gate: bfloat16 [512, 512], P(None, 'tensor'), may hold values from -0.25 to 0.25
- first_bias: float32 [512], P('tensor'), may hold values from -4 to 4
- second_bias: float32 [512], P('tensor'), may hold values from -4 to 4
- first_gain: float32 [512], replicated, may hold values from 0.5 to 1.5
- first_shift: float32 [512], replicated, may hold values from -2 to 2
- second_gain: float32 [512], replicated, may hold values from 0.5 to 1.5
- second_shift: float32 [512], replicated, may hold values from -2 to 2
Outputs:
- layer_output: bfloat16 [16384, 512], P('batch', 'tensor')
- input_gradient: float32 [16384, 512], P('batch', 'tensor')
- query_gradient: float32 [512, 512], P(None, 'tensor')
- key_gradient: float32 [512, 512], P(None, 'tensor')
- value_gradient: float32 [512, 512], P(None, 'tensor')
- output_gradient: float32 [512, 512], P('tensor')
- up_gradient: float32 [512, 2048], P(None, 'tensor')
- down_gradient: float32 [2048, 512], P('tensor')
- first_gate_gradient: float32 [512, 512], P(None, 'tensor')
- second_gate_gradient: float32 [512, 512], P(None, 'tensor')
- first_bias_gradient: float32 [512], P('tensor')
- second_bias_gradient: float32 [512], P('tensor')
- first_gain_gradient: float32 [512], replicated
- first_shift_gradient: float32 [512], replicated
- second_gain_gradient: float32 [512], replicated
- second_shift_gradient: float32 [512], replicated
- gate_stats: float32 [4], replicated
The draws below stay inside these ranges and needn't reach their ends.
All inputs are finite; a program needn't handle non-finite values.
Results may differ from the reference program's by a relative error of at most 0.012.
Values may be sent and summed in bfloat16 or wider, within the bound.
A program may use at most 128 MiB of HBM per device.

```python
import math
import jax
import jax.numpy as jnp
from jax import lax

D = 512
HEADS = 8
HD = 64
FF = 2048
LEN = 1024
TOKENS = 16384


def shard_levels(rng, dims, pieces, smallest, largest):
    def one(axis_at, shards_of):
        steps = jax.random.uniform(jax.random.fold_in(jax.random.fold_in(rng, 6), axis_at), (shards_of,), jnp.float32, smallest / len(pieces), largest / len(pieces))
        return jnp.repeat(jnp.exp(steps), dims[axis_at] // shards_of).reshape((-1,) + (1,) * (len(dims) - axis_at - 1))

    level = one(*pieces[0])
    for cut in pieces[1:]:
        level = level * one(*cut)
    return level


def gaussian(rng, dims, spread, bound, cuts=(), dtype=jnp.bfloat16):
    array = spread * jax.random.normal(rng, dims, jnp.float32)
    if cuts:
        array = array * shard_levels(rng, dims, cuts, -0.22, 0.18)
    return jnp.clip(array, -bound, bound).astype(dtype)


def setup_inputs(seed: int = 0) -> dict:
    keys = jax.random.split(jax.random.key(seed), 17)
    return {
        "tokens": gaussian(keys[0], (TOKENS, D), 1.0, 6.0, ((0, 8), (1, 4))),
        "cotangent": gaussian(keys[1], (TOKENS, D), 1.0, 6.0, ((0, 8), (1, 4)), jnp.float32),
        "query_weight": gaussian(keys[2], (D, D), D ** -0.5, 0.25, ((1, 4),)),
        "key_weight": gaussian(keys[3], (D, D), D ** -0.5, 0.25, ((1, 4),)),
        "value_weight": gaussian(keys[4], (D, D), D ** -0.5, 0.25, ((1, 4),)),
        "output_weight": gaussian(keys[5], (D, D), HD ** -0.5, 0.75, ((0, 4),)),
        "up_weight": gaussian(keys[6], (D, FF), D ** -0.5, 0.25, ((1, 4),)),
        "down_weight": gaussian(keys[7], (FF, D), FF ** -0.5, 0.125, ((0, 4),)),
        "first_gate": gaussian(keys[8], (D, D), D ** -0.5, 0.25, ((1, 4),)),
        "second_gate": gaussian(keys[9], (D, D), D ** -0.5, 0.25, ((1, 4),)),
        "first_bias": gaussian(keys[10], (D,), 1.0, 4.0, ((0, 4),), jnp.float32),
        "second_bias": gaussian(keys[11], (D,), 1.0, 4.0, ((0, 4),), jnp.float32),
        "first_gain": jnp.clip(1.0 + 0.1 * jax.random.normal(keys[12], (D,), jnp.float32), 0.5, 1.5),
        "first_shift": gaussian(keys[13], (D,), 0.3, 2.0, (), jnp.float32),
        "second_gain": jnp.clip(1.0 + 0.1 * jax.random.normal(keys[14], (D,), jnp.float32), 0.5, 1.5),
        "second_shift": gaussian(keys[15], (D,), 0.3, 2.0, (), jnp.float32),
    }


EPSILON = 1e-05
HIGHEST = lax.Precision.HIGHEST

@jax.custom_vjp
def low(v):
    return lax.optimization_barrier(v.astype(jnp.bfloat16)).astype(jnp.float32)

@jax.custom_vjp
def low_back(v):
    return v

def low_keep(v):
    return (low(v), None)

def low_pass(kept, grad):
    return (grad,)

def back_keep(v):
    return (v, None)

def back_low(kept, grad):
    return (low(grad),)
low.defvjp(low_keep, low_pass)
low_back.defvjp(back_keep, back_low)

def matmul(left, right):
    return jnp.dot(left, right, precision=HIGHEST, preferred_element_type=jnp.float32)

def normalize(values, gain, shift):
    centred = values - lax.optimization_barrier(jnp.mean(values, axis=-1, keepdims=True))
    variance = lax.optimization_barrier(jnp.mean(centred * centred, axis=-1, keepdims=True))
    return centred * lax.rsqrt(variance + EPSILON) * gain + shift

def attend_window(triple):
    query_rows, key_rows, value_rows = triple
    scaling = 1.0 / math.sqrt(HD)
    raw = jnp.einsum('qhd,khd->hqk', query_rows, key_rows, precision=HIGHEST) * scaling
    raw = low_back(raw)
    places = jnp.arange(LEN)
    causal = places[:, None] >= places[None, :]
    scores = jnp.where(causal[None], raw, -1e+30)
    probs = jax.nn.softmax(scores, axis=-1)
    return jnp.einsum('hqk,khd->qhd', low(probs), value_rows, precision=HIGHEST)

def forward(inputs, query_weight, key_weight, value_weight, output_weight, up_weight, down_weight, first_gate, second_gate, first_bias, second_bias, first_gain, first_shift, second_gain, second_shift):
    first_normed = low(normalize(inputs, first_gain, first_shift))

    def project(weight):
        return low(low_back(matmul(first_normed, weight))).reshape(-1, LEN, HEADS, HD)
    queries, keys_all, values_all = (project(query_weight), project(key_weight), project(value_weight))
    attended = lax.map(jax.checkpoint(attend_window), (queries, keys_all, values_all))
    attended = low(low_back(attended.reshape(-1, D)))
    attn_branch = low_back(matmul(attended, output_weight))
    attn_gate = jax.nn.sigmoid(low_back(matmul(first_normed, first_gate) + first_bias))
    middle = inputs + attn_gate * attn_branch
    second_normed = low(normalize(middle, second_gain, second_shift))
    pre_hidden = low_back(matmul(second_normed, up_weight))
    hidden = low(jax.nn.gelu(pre_hidden, approximate=True))
    ffn_branch = low_back(matmul(hidden, down_weight))
    ffn_gate = jax.nn.sigmoid(low_back(matmul(second_normed, second_gate) + second_bias))
    return (middle + ffn_gate * ffn_branch, (attn_gate, ffn_gate))

def reference(tokens, cotangent, query_weight, key_weight, value_weight, output_weight, up_weight, down_weight, first_gate, second_gate, first_bias, second_bias, first_gain, first_shift, second_gain, second_shift):
    floats = [item.astype(jnp.float32) for item in (tokens, query_weight, key_weight, value_weight, output_weight, up_weight, down_weight, first_gate, second_gate, first_bias, second_bias, first_gain, first_shift, second_gain, second_shift)]
    result, pullback, gates = jax.vjp(forward, *floats, has_aux=True)
    grads = pullback(cotangent.astype(jnp.float32))
    attn_gate, ffn_gate = gates
    first_mean = jnp.mean(attn_gate)
    second_mean = jnp.mean(ffn_gate)
    gate_stats = jnp.stack([first_mean, jnp.mean(attn_gate * attn_gate) - first_mean * first_mean, second_mean, jnp.mean(ffn_gate * ffn_gate) - second_mean * second_mean])
    return (result.astype(jnp.bfloat16), grads[0], grads[1], grads[2], grads[3], grads[4], grads[5], grads[6], grads[7], grads[8], grads[9], grads[10], grads[11], grads[12], grads[13], grads[14], gate_stats)
```

```python
import functools
import math

import jax
import jax.numpy as jnp
from jax import lax
from jax.experimental import pallas as pl
from jax.experimental.pallas import tpu as pltpu
from jax.sharding import PartitionSpec as P

F32 = jnp.float32
BF16 = jnp.bfloat16
D = 512
LEN = 1024
OWN = 512
QB = 256
LANE = 128
EPSILON = 1e-05
GELU_C = math.sqrt(2.0 / math.pi)
MESH = pl.DeviceIdType.MESH

DOWN, UP, GATE2, WO, GATE1, QKV, ROWS = 0, 2048, 4096, 4608, 5120, 5632, 7168

ORDER = (
    "down:p3", "do:gate2", "down_a", "hidden:p3", "down:p1", "gate2", "down:p2", "up:p3",
    "hidden:p1", "hidden:t", "down_b", "down:t", "down_b", "down_a", "up_a", "gate2", "up:p1",
    "up_a", "down_a", "hidden:p2", "do:middle", "up:p2", "down_b", "up_b", "up:t", "do:output",
    "up_a", "far:0", "output", "up_b", "down_a", "far:1", "far:2", "output", "down_b", "gate2",
    "up_b", "down_a", "up_a", "far:3", "far:end", "up_b", "gate2", "own:0", "far:project",
    "down_a", "own:1", "down_b", "key", "up_a", "value", "gate2", "output", "up_b", "query",
    "own:2", "up_a", "own:3", "down_b", "own:end", "do:other", "own:project", "up_b", "key",
    "value", "up_a", "query", "down_a", "output", "down_b", "key", "do:own", "gate2", "value",
    "output", "do:norm", "sums", "down_b", "give_in", "up_a", "key", "query", "value", "down_a",
    "output", "up_b", "down_b", "up_a", "key", "sums", "gate2", "give_out", "query", "output",
    "key", "sums", "up_b", "value", "query", "output", "key", "up_a", "value", "query", "down_b",
    "sums", "output", "key",
)


def mm(a, b):
    return jnp.dot(a, b, preferred_element_type=F32)


def mm_nt(a, b):
    return lax.dot_general(a, b, (((1,), (1,)), ((), ())), preferred_element_type=F32)


def mm_tn(a, b):
    return lax.dot_general(a, b, (((0,), (0,)), ((), ())), preferred_element_type=F32)


def at(start, size, step=LANE):
    return pl.ds(pl.multiple_of(start, step), size)


def repeat(start, stop, step):
    for i in range(start, stop):
        step(i)


def colsum(v):
    return jnp.sum(v, axis=0, keepdims=True)


def unit(x):
    centred = x - jnp.mean(x, axis=-1, keepdims=True)
    recip = lax.rsqrt(jnp.mean(centred * centred, axis=-1, keepdims=True) + EPSILON)
    return centred * recip, recip


def layer_kernel(
    nb,
    tok, cot, wq, wk, wv, wo, up, dn, g1, g2, b1, b2, ga1, sh1, ga2, sh2,
    lo, ig, fin_o, small_o,
    xs, n1, n1t, wqkv, wo_f, g1_f, g2_f, up_f, dn_f, bias, cotf, cots, cotr,
    qkv, pr, attw, att, mid, ab, ag, n2, n2t, hid, gp, facc, gfb, gfl, gn2, gm, gab, gal,
    gatt, gaw, dvt, dkt, dqkv, gin, gins, ginr, los, igs,
    gr, l1, lx, fin, sums, smb, sml, smt,
    send_sems, recv_sems, local_sems,
):
    t = lax.axis_index("tensor")
    b = lax.axis_index("batch")
    c = t % 2
    y = t // 2
    p1 = t + 1 - 2 * c
    p2 = t + 2 - 4 * y
    p3 = p1 + 2 - 4 * y
    nbits = nb.bit_length() - 1
    nh = min(3, nbits)
    bits = [(b // (1 << k)) % 2 for k in range(nbits)]
    steps_to = [(1 << k) * (1 - 2 * bits[k]) for k in range(nbits)]
    peers = [b + steps_to[k] for k in range(nbits)]
    cube = [
        (b + sum(steps_to[k] for k in range(nh) if (mask >> k) % 2), t)
        for mask in range(1, 1 << nh)
    ]

    sent = []
    local = []

    def send(src, dst, dev):
        k = len(sent)
        copy = pltpu.make_async_remote_copy(
            src_ref=src, dst_ref=dst, send_sem=send_sems.at[k], recv_sem=recv_sems.at[k],
            device_id=dev, device_id_type=MESH,
        )
        copy.start()
        sent.append(copy)
        return copy

    finished = set()

    def finish(copy):
        if id(copy) not in finished:
            finished.add(id(copy))
            copy.wait_send()

    def fetch(src, dst):
        copy = pltpu.make_async_copy(src, dst, local_sems.at[len(local)])
        copy.start()
        local.append(copy)
        return copy

    d1, d2, d3 = (b, p1), (b, p2), (b, p3)

    win = at(y * LEN, LEN)

    def qkv_blocks(slot):
        return [wqkv.at[:, at(slot * 384 + j * LANE, LANE)] for j in range(3)]

    def mid_blocks(q):
        return [wo_f.at[at(q * LANE, LANE)], g1_f.at[:, at(q * LANE, LANE)]]

    def up_blocks(q):
        return [up_f.at[q], g2_f.at[:, at(q * LANE, LANE)]]

    def piece(ref):
        rows = ref.shape[0] >> min(2, nbits)
        return ref.at[at(sum(bits[k] * (rows << k) for k in range(min(2, nbits))), rows, 32)]

    got_tok = fetch(tok.at[win], xs.at[t])
    got_qkv = [fetch(w, dst) for w, dst in zip((wq, wk, wv), qkv_blocks(y))]
    got_cot = fetch(cot, cotf)
    got_mid = [fetch(w, dst) for w, dst in zip((wo, g1), mid_blocks(t))]
    got_ffn = [fetch(w, dst) for w, dst in zip((up, g2, dn), up_blocks(t) + [dn_f.at[t]])]

    barrier = pltpu.get_barrier_semaphore()
    partners = [d1, d2, d3] + cube + [(peer, t) for peer in peers[nh:]]
    for dev in partners:
        pl.semaphore_signal(barrier, inc=1, device_id=dev, device_id_type=MESH)
    pl.semaphore_wait(barrier, len(partners))

    square = cube[:(1 << min(2, nbits)) - 1]

    def over_y(blocks, refs):
        return [send(piece(w), piece(dst), d2) for w, dst in zip(blocks, refs)]

    def over_square(copies, refs):
        for copy in copies:
            copy.wait_recv()
        return [send(piece(ref), piece(ref), dev) for ref in refs for dev in square]

    def over_core(copies, refs):
        for copy in copies:
            copy.wait_recv()
        return [send(ref, ref, d1) for ref in refs]

    def token_half(i):
        rows = pl.ds(i * OWN, OWN)
        return send(tok.at[at((1 - y) * LEN + i * OWN, OWN)], xs.at[t, rows], d2)

    qkv_y = over_y((wq, wk, wv), qkv_blocks(y))
    tok_2 = [token_half(0), token_half(1)]
    tok_1 = send(tok.at[win], xs.at[t], d1)
    bias[t, 0:1, :] = b1[...]
    bias[t, 1:2, :] = b2[...]
    bias_x = [send(bias.at[t], bias.at[t], dev) for dev in (d1, d2, d3)]
    mid_1 = [send(w, dst, d1) for w, dst in zip((wo, g1), mid_blocks(t))]

    qkv_s = over_square(qkv_y, qkv_blocks(1 - y))
    up_y = over_y((up, g2), up_blocks(t))
    got_cot.wait()

    def to_low(i, carry):
        rows = at(i * QB, QB)
        cots[rows] = cotf[rows].astype(BF16)
        return carry

    lax.fori_loop(0, 4 * OWN // QB, to_low, 0)
    cotr[t] = cots[at(t * OWN, OWN)]
    def pass_tokens(i):
        rows = pl.ds(i * OWN, OWN)
        tok_2[i].wait_recv()
        return send(xs.at[p2, rows], xs.at[p2, rows], d1)

    tok_3 = [pass_tokens(0), pass_tokens(1)]
    mid_y = over_y((wo, g1), mid_blocks(t))
    dn_y = [send(dn, dn_f.at[t], d2)]
    ffn_1 = [send(w, dst, d1) for w, dst in zip((up, g2, dn), up_blocks(t) + [dn_f.at[t]])]

    def tokens_at(rows):
        return jnp.concatenate([xs[j, rows, :].astype(F32) for j in range(4)], axis=1)

    def first_norm(i):
        rows = at(i * QB, QB)
        u, _ = unit(tokens_at(rows))
        n1[rows, :] = (u * ga1[...] + sh1[...]).astype(BF16)

    got_tok.wait()
    tok_1.wait_recv()
    tok_3[0].wait_recv()
    repeat(0, OWN // QB, first_norm)
    up_s = over_square(up_y, up_blocks(p2))
    tok_3[1].wait_recv()
    repeat(OWN // QB, LEN // QB, first_norm)

    for copy in got_qkv:
        copy.wait()
    for copy in qkv_s:
        copy.wait_recv()

    def project(i):
        rows = at(i * QB, QB)
        out = mm(n1[rows, :], wqkv[...])
        for s in range(2):
            base = s * 384
            qkv[rows, base:base + LANE] = (out[:, base:base + LANE].astype(BF16) * 0.125).astype(BF16)
            qkv[rows, base + LANE:base + 384] = out[:, base + LANE:base + 384].astype(BF16)

    repeat(0, LEN // QB, project)

    lane = lax.broadcasted_iota(jnp.int32, (1, LANE), 1)
    heads = [lane < 64, lane >= 64]
    heads_low = [jnp.where(h, 1.0, 0.0).astype(BF16) for h in heads]
    causal = lax.broadcasted_iota(jnp.int32, (QB, QB), 0) >= lax.broadcasted_iota(
        jnp.int32, (QB, QB), 1
    )

    def attend(s):
        base = s * 384
        for i in range(LEN // QB):
            rows = pl.ds(i * QB, QB)
            query = qkv[rows, at(base, LANE)]
            outs = []
            for h in range(2):
                masked = query * heads_low[h]
                near = mm_nt(masked, qkv[rows, at(base + LANE, LANE)])
                near = jnp.where(causal, near, -1e30)
                peak = jnp.max(near, axis=-1, keepdims=True)
                if i > 0:
                    far = mm_nt(masked, qkv[0:i * QB, at(base + LANE, LANE)])
                    peak = jnp.maximum(peak, jnp.max(far, axis=-1, keepdims=True))
                    far = jnp.exp(far - peak)
                near = jnp.exp(near - peak)
                total = jnp.sum(near, axis=-1, keepdims=True)
                if i > 0:
                    total = total + jnp.sum(far, axis=-1, keepdims=True)
                scale = 1.0 / total
                near = (near * scale).astype(BF16)
                pr[s * 2 + h, rows, i * QB:(i + 1) * QB] = near
                out = mm(near, qkv[rows, at(base + 2 * LANE, LANE)])
                if i > 0:
                    far = (far * scale).astype(BF16)
                    pr[s * 2 + h, rows, 0:i * QB] = far
                    out = out + mm(far, qkv[0:i * QB, at(base + 2 * LANE, LANE)])
                outs.append(out)
            attw[rows, at(s * LANE, LANE)] = jnp.where(heads[0], outs[0], outs[1]).astype(BF16)
    own_w = at(c * OWN, OWN)
    other_w = at((1 - c) * OWN, OWN)
    att_x = []
    moved = {"mid": over_square(mid_y, mid_blocks(p2))}

    for s in range(2):
        attend(s)
        cols = at((c + 2 * s) * LANE, LANE)
        att_x.append(send(attw.at[other_w, pl.ds(s * LANE, LANE)], att.at[:, cols], d1))
        att[:, cols] = attw[own_w, pl.ds(s * LANE, LANE)]

    moved["mid"] = over_core(moved["mid"], mid_blocks(p2))
    dn_3 = over_core(dn_y, (dn_f.at[p2],))
    cot_x = [
        send(cots.at[at(p * OWN, OWN)], cotr.at[t], dev)
        for p, dev in ((p1, d1), (p2, d2), (p3, d3))
    ]
    up_3 = over_core(up_s, up_blocks(p2))
    for copy in got_mid:
        copy.wait()
    for copy in mid_1 + moved["mid"] + bias_x + att_x:
        copy.wait_recv()

    sums[...] = jnp.zeros((16, D), F32)

    def note(row, value):
        sums[row:row + 1, :] += value

    def row_of(j):
        return jnp.concatenate([bias[k, j:j + 1, :] for k in range(4)], axis=1)

    def first_branch(i):
        rows = at(i * QB, QB)
        wrows = at(c * OWN + i * QB, QB)
        branch = mm(att[rows, :], wo_f[...])
        gate = jax.nn.sigmoid(mm(n1[wrows, :], g1_f[...]) + row_of(0))
        middle = tokens_at(wrows) + gate * branch
        ab[rows, :] = branch
        ag[rows, :] = gate
        mid[rows, :] = middle
        u, _ = unit(middle)
        n2[rows, :] = (u * ga2[...] + sh2[...]).astype(BF16)
        note(6, colsum(gate))
        note(7, colsum(gate * gate))

    repeat(0, OWN // QB, first_branch)

    for copy in got_ffn:
        copy.wait()

    def forward_up(q):
        for i in range(OWN // QB):
            rows = pl.ds(i * QB, QB)
            pre = mm(n2[rows, :], up_f[q])
            square = pre * pre
            th = jnp.tanh(pre * (GELU_C + (0.044715 * GELU_C) * square))
            share = 0.5 + 0.5 * th
            hidden = pre * share
            hid[q, rows, :] = hidden.astype(BF16)
            tilt = hidden * (1.0 - share)
            slope = share + tilt * (2.0 * GELU_C + (0.26829 * GELU_C) * square)
            gp[q, rows, :] = slope.astype(BF16)

    def forward_down(one, two, first):
        for i in range(OWN // QB):
            rows = pl.ds(i * QB, QB)
            part = mm(hid[one, rows, :], dn_f[one]) + mm(hid[two, rows, :], dn_f[two])
            facc[rows, :] = part if first else facc[rows, :] + part

    forward_up(t)
    for copy in ffn_1:
        copy.wait_recv()
    forward_up(p1)
    forward_down(t, p1, True)
    forward_up(p2)
    for copy in up_3:
        copy.wait_recv()
    forward_up(p3)
    for copy in dn_3:
        copy.wait_recv()
    forward_down(p2, p3, False)

    for copy in cot_x:
        copy.wait_recv()

    def cot_at(rows):
        return jnp.concatenate([cotr[j, rows, :].astype(F32) for j in range(4)], axis=1)

    def second_branch(i):
        rows = at(i * QB, QB)
        branch = facc[rows, :]
        gate = jax.nn.sigmoid(mm(n2[rows, :], g2_f[...]) + row_of(1))
        out = (mid[rows, :] + gate * branch).astype(BF16)
        for j in range(4):
            los[j, rows, :] = out[:, j * LANE:(j + 1) * LANE]
        grad = cot_at(rows)
        gfb[rows, :] = (grad * gate).astype(BF16)
        logit = (grad * branch * gate * (1.0 - gate)).astype(BF16)
        gfl[rows, :] = logit
        note(5, colsum(logit.astype(F32)))
        note(8, colsum(gate))
        note(9, colsum(gate * gate))

    repeat(0, OWN // QB, second_branch)

    mine = at(t * OWN, OWN)

    def give_back(blocks, out):
        fetch(blocks.at[t], out.at[mine])
        return [send(blocks.at[p], out.at[mine], dev) for p, dev in ((p1, d1), (p2, d2), (p3, d3))]

    landing = [0]

    def land(size):
        start = landing[0]
        landing[0] += size
        return start

    def sum_rows(dst, q, base, off, size, terms):
        if not terms:
            return
        chunk = next(n for n in (256, 128, 64) if size % n == 0)

        def step(i, carry):
            here = off + i * chunk
            rows = at(base + here, chunk, 32)
            total = gr[q, rows, :].astype(F32)
            for ref, start in terms:
                total = total + ref[at(start + here, chunk, 32), :].astype(F32)
            dst[rows, :] = total.astype(BF16)
            return carry

        lax.fori_loop(0, size // chunk, step, 0)

    def place(dims, mask):
        return sum(
            (1 << k) * (1 - bits[dim] if (mask >> k) % 2 else bits[dim])
            for k, dim in enumerate(dims)
        )

    def peer_of(dims, mask):
        return (b + sum(steps_to[dim] for k, dim in enumerate(dims) if (mask >> k) % 2), t)

    def reduce_stages(base, size, order, terms):
        off, span = 0, size
        quarters = [("far", p2), ("own", t)]
        for dim in order:
            copies = []
            if dim == "y":
                quarters = quarters[1:]
                sum_rows(gr.at[p2], p2, base, off, span, terms["far"])
                start = land(span)
                rows = at(base + off, span, 32)
                copies.append(send(gr.at[p2, rows], lx.at[pl.ds(start, span)], d2))
                terms["own"] = terms["own"] + [(lx, start - off)]
                yield copies
                continue
            if isinstance(dim, tuple):
                span = span >> len(dim)
                keep = off + place(dim, 0) * span
                for mask in range(1, 1 << len(dim)):
                    away = off + place(dim, mask) * span
                    sum_rows(gr.at[t], t, base, away, span, terms["own"])
                    copies.append((mask, away))
                landed = []
                for k, (mask, away) in enumerate(copies):
                    start = land(span)
                    rows = at(base + away, span, 32)
                    copies[k] = send(gr.at[t, rows], lx.at[pl.ds(start, span)], peer_of(dim, mask))
                    landed.append((lx, start - keep))
                terms["own"] = terms["own"] + landed
                off = keep
                yield copies
                continue
            span = span // 2
            keep = off + bits[dim] * span
            away = off + (1 - bits[dim]) * span
            for name, q in quarters:
                sum_rows(gr.at[q], q, base, away, span, terms[name])
                start = land(span)
                rows = at(base + away, span, 32)
                copies.append(send(gr.at[q, rows], lx.at[pl.ds(start, span)], (peers[dim], t)))
                terms[name] = terms[name] + [(lx, start - keep)]
            off = keep
            yield copies
        for dim in range(nh, nbits):
            sum_rows(gr.at[t], t, base, off, span, terms["own"])
            start = land(span)
            rows = at(base + off, span, 32)
            copy = send(gr.at[t, rows], lx.at[pl.ds(start, span)], (peers[dim], t))
            yield [copy]
            finish(copy)
            terms["own"] = [(lx, start - off)]
        sum_rows(fin, t, base, off, span, terms["own"])
        for dim in reversed([dim for dim in order if dim != "y"]):
            part = fin.at[at(base + off, span, 32)]
            if isinstance(dim, tuple):
                masks = range(1, 1 << len(dim))
                yield [send(part, part, peer_of(dim, mask)) for mask in masks]
                off = off - place(dim, 0) * span
                span = span << len(dim)
                continue
            yield [send(part, part, (peers[dim], t))]
            off = off - bits[dim] * span
            span = span * 2
        fetch(fin.at[pl.ds(base, size)], fin_o.at[pl.ds(base, size)])

    def waiting(stages):
        for copies in stages:
            yield
            for copy in copies:
                copy.wait_recv()

    def batch_order(*dims):
        order = []
        for dim in dims:
            if isinstance(dim, tuple):
                dim = tuple(d for d in dim if d < nh)
                dim = dim if len(dim) > 1 else dim[0] if dim else nh
            if isinstance(dim, tuple) or dim == "y" or dim < nh:
                order.append(dim)
        if dims[0] != "y" and order[0] == "y":
            order[:2] = order[1::-1]
        return order

    def gradient_chain(base, size, order, split):
        rows = pl.ds(base, size)
        far = send(gr.at[p3, rows], l1.at[1, rows], d1)
        if split:
            yield
        y_first = order[0] == "y"
        if y_first and split:
            own = []
        else:
            own = [send(gr.at[p1, rows], l1.at[0, rows], d1)]
            yield
        far.wait_recv()
        if not y_first:
            own[0].wait_recv()
        terms = {"far": [(l1.at[1], base)], "own": [(l1.at[0], base)]}
        stages = waiting(reduce_stages(base, size, order, terms))
        if y_first:
            next(stages)
            yield
            if split:
                own = [send(gr.at[p1, rows], l1.at[0, rows], d1)]
                yield
            own[0].wait_recv()
        yield from stages

    def last_gradients(base, size, order):
        yield from waiting(reduce_stages(base, size, order, {"far": [], "own": []}))

    def sum_chain():
        copies = [
            send(sums.at[:, at(p * LANE, LANE)], sml.at[k], dev)
            for k, (p, dev) in enumerate(((p1, d1), (p2, d2), (p3, d3)))
        ]
        yield
        for copy in copies:
            copy.wait_recv()
        smb[0] = sums[:, at(t * LANE, LANE)] + sml[0] + sml[1] + sml[2]
        copies = [send(smb.at[0], sml.at[3 + k], dev) for k, dev in enumerate(cube)]
        yield
        for copy in copies:
            copy.wait_recv()
        total = smb[0]
        for k in range(len(cube)):
            total = total + sml[3 + k]
        place_now = 3 + len(cube)
        for k in range(nh, nbits):
            smb[k - nh + 1] = total
            copy = send(smb.at[k - nh + 1], sml.at[place_now], (peers[k], t))
            yield
            copy.wait_recv()
            total = total + sml[place_now]
            place_now += 1
        smt[t] = total
        copies = [send(smt.at[t], smt.at[t], dev) for dev in (d1, d2, d3)]
        yield
        for copy in copies:
            copy.wait_recv()
        fetch(smt, small_o)

    returned = []

    def give_chain(blocks, out):
        returned.extend(give_back(blocks, out))
        yield

    chains = {
        "down_a": gradient_chain(DOWN, 1024, batch_order("y", 0, (1, 2)), True),
        "down_b": gradient_chain(DOWN + 1024, 1024, batch_order(0, "y", 1, 2), True),
        "up_a": gradient_chain(UP, 1024, batch_order(1, "y", 0, 2), True),
        "up_b": gradient_chain(UP + 1024, 1024, batch_order("y", 0, (1, 2)), True),
        "gate2": gradient_chain(GATE2, D, batch_order(0, "y", (1, 2)), False),
        "output": gradient_chain(WO, QKV - WO, batch_order(1, 0, "y", 2), False),
        "query": last_gradients(QKV, D, batch_order("y", 0, (1, 2))),
        "key": last_gradients(QKV + D, D, batch_order("y", 0, 1, 2)),
        "value": last_gradients(QKV + 2 * D, D, batch_order("y", (0, 1), 2)),
        "sums": sum_chain(),
        "give_out": give_chain(los, lo),
        "give_in": give_chain(igs, ig),
    }

    def gradient_rows(q, base, i, grad):
        for j in range(grad.shape[1] // LANE):
            gr[q, pl.ds(base + j * D + i * QB, QB), :] = grad[:, j * LANE:(j + 1) * LANE]

    def down_gradient(q):
        for i in range(2):
            grad = mm_tn(hid[q, :, i * QB:(i + 1) * QB], gfb[...]).astype(BF16)
            gradient_rows(q, DOWN, i, grad)

    done = set()

    def once(name):
        new = name not in done
        done.add(name)
        return new

    def turn_second():
        if once("n2t"):
            n2t[...] = n2[...].T

    def turn_first():
        if once("n1t"):
            for i in range(LEN // QB):
                n1t[:, i * QB:(i + 1) * QB] = n1[i * QB:(i + 1) * QB, :].T

    def hidden_back(q):
        first = once("gn2")
        for i in range(OWN // QB):
            rows = pl.ds(i * QB, QB)
            grad = mm_nt(gfb[rows, :], dn_f[q])
            pre = (grad * gp[q, rows, :].astype(F32)).astype(BF16)
            gp[q, rows, :] = pre
            part = mm_nt(pre, up_f[q])
            gn2[rows, :] = part if first else gn2[rows, :] + part

    def up_gradient(q):
        turn_second()
        for i in range(2):
            gradient_rows(q, UP, i, mm(n2t[i * QB:(i + 1) * QB, :], gp[q]).astype(BF16))

    def gate_gradient(left, right, base):
        for i in range(2):
            grad = mm(left(slice(i * QB, (i + 1) * QB)), right[...]).astype(BF16)
            for j in range(4):
                gr[j, pl.ds(base + i * QB, QB), :] = grad[:, j * LANE:(j + 1) * LANE]

    def second_gate_gradient():
        turn_second()
        gate_gradient(lambda cols: n2t[cols, :], gfl, GATE2)

    def second_back(i):
        rows = at(i * QB, QB)
        grad = gn2[rows, :] + mm_nt(gfl[rows, :], g2_f[...])
        u, recip = unit(mid[rows, :])
        s = grad * ga2[...]
        through = recip * (
            s - jnp.mean(s, axis=-1, keepdims=True) - u * jnp.mean(s * u, axis=-1, keepdims=True)
        )
        total = cot_at(rows) + through
        gm[rows, :] = total
        note(2, colsum(grad * u))
        note(3, colsum(grad))
        gate = ag[rows, :]
        low = (total * gate).astype(BF16)
        gab[rows, :] = low
        logit = (total * ab[rows, :] * gate * (1.0 - gate)).astype(BF16)
        gal[rows, :] = logit
        note(4, colsum(logit.astype(F32)))
        gatt[rows, :] = mm_nt(low, wo_f[...]).astype(BF16)

    exchanged = {}

    def middle_back():
        repeat(0, OWN // QB, second_back)
        for name, q, slot in (("far", p3, 1 - y), ("own", p1, y)):
            exchanged[name] = send(
                gatt.at[:, at(q * LANE, LANE)], gaw.at[own_w, at(slot * LANE, LANE)], d1
            )
        for q, slot in ((p2, 1 - y), (t, y)):
            gaw[own_w, at(slot * LANE, LANE)] = gatt[:, at(q * LANE, LANE)]

    def output_gradient():
        turn_first()
        gate_gradient(lambda cols: n1t[cols, own_w], gal, GATE1)
        for i in range(2):
            outer = mm_tn(att[:, i * QB:(i + 1) * QB], gab[...]).astype(BF16)
            for k in range(2):
                for j in range(4):
                    gr[2 * i + k, pl.ds(WO + j * LANE, LANE), :] = outer[
                        k * LANE:(k + 1) * LANE, j * LANE:(j + 1) * LANE
                    ]

    slots = {"far": 1 - y, "own": y}

    def block_back(name, i):
        if i == 0:
            exchanged[name].wait_recv()
        s = slots[name]
        base = s * 384
        rows = pl.ds(i * QB, QB)
        reach = (i + 1) * QB
        query = qkv[rows, at(base, LANE)]
        grad = gaw[rows, at(s * LANE, LANE)]
        prod = grad.astype(F32) * attw[rows, at(s * LANE, LANE)].astype(F32)
        outs = []
        for h in range(2):
            masked = grad * heads_low[h]
            delta = jnp.sum(jnp.where(heads[h], prod, 0.0), axis=-1, keepdims=True)
            probs = pr[s * 2 + h, rows, 0:reach]
            dprobs = mm_nt(masked, qkv[0:reach, at(base + 2 * LANE, LANE)])
            scores = (probs.astype(F32) * (dprobs - delta)).astype(BF16)
            outs.append(mm(scores, qkv[0:reach, at(base + LANE, LANE)]))
            value_part = mm_tn(masked, probs)
            key_part = mm_tn(query * heads_low[h], scores)
            if h == 0:
                dvt[:, i * QB:reach] = value_part[:, i * QB:reach]
                dkt[:, i * QB:reach] = key_part[:, i * QB:reach]
                if i > 0:
                    dvt[:, 0:i * QB] += value_part[:, 0:i * QB]
                    dkt[:, 0:i * QB] += key_part[:, 0:i * QB]
            else:
                dvt[:, 0:reach] += value_part
                dkt[:, 0:reach] += key_part
        dqkv[rows, at(base, LANE)] = (jnp.where(heads[0], outs[0], outs[1]) * 0.125).astype(BF16)

    def blocks_end(name):
        base = slots[name] * 384
        for i in range(LEN // QB):
            rows = pl.ds(i * QB, QB)
            dqkv[rows, at(base + LANE, LANE)] = dkt[:, i * QB:(i + 1) * QB].T.astype(BF16)
            dqkv[rows, at(base + 2 * LANE, LANE)] = dvt[:, i * QB:(i + 1) * QB].T.astype(BF16)

    def project_back(name):
        turn_first()
        q = {"far": p2, "own": t}[name]
        for i in range(2):
            grad = mm(n1t[i * QB:(i + 1) * QB, :], dqkv[:, at(slots[name] * 384, 384)])
            gradient_rows(q, QKV, i, grad.astype(BF16))

    def back_to_other():
        for i in range(OWN // QB):
            rows = at((1 - c) * OWN + i * QB, QB)
            gins[pl.ds(i * QB, QB), :] = mm_nt(dqkv[rows, :], wqkv[...]).astype(BF16)
        exchanged["in"] = send(gins, ginr, d1)

    def back_to_own():
        for i in range(OWN // QB):
            rows = pl.ds(i * QB, QB)
            gin[rows, :] = mm_nt(dqkv[at(c * OWN + i * QB, QB), :], wqkv[...]) + mm_nt(
                gal[rows, :], g1_f[...]
            )

    def first_back(i):
        rows = at(i * QB, QB)
        grad = gin[rows, :] + ginr[rows, :].astype(F32)
        u, recip = unit(tokens_at(at(c * OWN + i * QB, QB)))
        s = grad * ga1[...]
        through = recip * (
            s - jnp.mean(s, axis=-1, keepdims=True) - u * jnp.mean(s * u, axis=-1, keepdims=True)
        )
        total = (gm[rows, :] + through).astype(BF16)
        for j in range(4):
            igs[j, rows, :] = total[:, j * LANE:(j + 1) * LANE]
        note(0, colsum(grad * u))
        note(1, colsum(grad))

    def norm_back():
        exchanged["in"].wait_recv()
        repeat(0, OWN // QB, first_back)

    quarters = {"p3": p3, "p2": p2, "p1": p1, "t": t}
    steps = {
        "gate2": second_gate_gradient, "middle": middle_back, "output": output_gradient,
        "other": back_to_other, "own": back_to_own, "norm": norm_back,
    }

    def compute(kind, what):
        if kind == "do":
            steps[what]()
        elif kind in slots:
            if what == "end":
                blocks_end(kind)
            elif what == "project":
                project_back(kind)
            else:
                block_back(kind, int(what))
        else:
            {"down": down_gradient, "hidden": hidden_back, "up": up_gradient}[kind](quarters[what])

    drained = [0]

    def drain(keep):
        while drained[0] < len(sent) - keep:
            finish(sent[drained[0]])
            drained[0] += 1

    def stage(name):
        if name in chains and next(chains[name], 0) == 0:
            del chains[name]
        drain(32)

    for name in ORDER:
        if ":" in name:
            compute(*name.split(":"))
        else:
            stage(name)
    while chains:
        for name in tuple(chains):
            stage(name)
    for copy in returned:
        copy.wait_recv()
    drain(0)
    for copy in local[10:]:
        copy.wait()


def spread_kernel(
    entries, lo, ig, fin, small,
    layer_output, input_gradient, query, key, value, output, upg, downg, gate1, gate2,
    bias1, bias2, gain1, shift1, gain2, shift2, stats,
    lo_v, ig_v, fin_v, small_v, ig_w, square_w, output_w, cols_w, bias_w, norm_w, stats_w,
    sems, out_sems,
):
    t = lax.axis_index("tensor")

    def pull(src, dst, k):
        copy = pltpu.make_async_copy(src, dst, sems.at[k])
        copy.start()
        return copy

    got_small = pull(small, small_v, 6)
    rows = [(DOWN, 2048), (UP, 2048), (GATE2, QKV - GATE2), (QKV, ROWS - QKV)]
    pieces = [
        pull(fin.at[pl.ds(r, n)], fin_v.at[pl.ds(r, n)], 1 + k) for k, (r, n) in enumerate(rows)
    ]
    got_ig = pull(ig, ig_v, 5)
    got_lo = pull(lo, lo_v, 0)
    pushed = []

    def push(src, dst):
        copy = pltpu.make_async_copy(src, dst, out_sems.at[len(pushed)])
        copy.start()
        pushed.append(copy)

    got_small.wait()
    for k, out in enumerate((bias1, bias2)):
        bias_w[k] = small_v[t, 4 + k:5 + k, :]
        push(bias_w.at[k], out)
    for row, out in enumerate((gain1, shift1, gain2, shift2)):
        for j in range(4):
            norm_w[row, :, j * LANE:(j + 1) * LANE] = small_v[j, row:row + 1, :]
        push(norm_w.at[row], out)
    means = [
        jnp.sum(sum(small_v[j, row:row + 1, :] for j in range(4)), axis=1, keepdims=True) / entries
        for row in range(6, 10)
    ]
    lane = lax.broadcasted_iota(jnp.int32, (1, LANE), 1)
    parts = [means[0], means[1] - means[0] * means[0], means[2], means[3] - means[2] * means[2]]
    row = jnp.zeros((1, LANE), F32)
    for j in range(4):
        row = jnp.where(lane == j, parts[j], row)
    stats_w[...] = row[:, 0:4]
    push(stats_w, stats)
    for k, (base, out) in enumerate(((DOWN, downg), (UP, upg))):
        pieces[k].wait()
        for j in range(4):
            square_w[k, :, j * LANE:(j + 1) * LANE] = fin_v[
                base + j * D:base + (j + 1) * D, :
            ].astype(F32)
        push(square_w.at[k], out)
    pieces[2].wait()
    for j in range(4):
        output_w[:, j * LANE:(j + 1) * LANE] = fin_v[
            WO + j * LANE:WO + (j + 1) * LANE, :
        ].astype(F32)
    push(output_w, output)
    for k, (base, out) in enumerate(
        ((GATE2, gate2), (GATE1, gate1), (QKV, query), (QKV + D, key), (QKV + 2 * D, value))
    ):
        if k == 2:
            pieces[3].wait()
        cols_w[k] = fin_v[base:base + D, :].astype(F32)
        push(cols_w.at[k], out)
    got_ig.wait()
    for k in range(2):
        half = pl.ds(k * 2 * OWN, 2 * OWN)
        ig_w[half, :] = ig_v[half, :].astype(F32)
        push(ig_w.at[half], input_gradient.at[half])
    got_lo.wait()
    push(lo_v, layer_output)
    for copy in pushed:
        copy.wait()


def per_device(
    nb, tokens, cotangent, query_weight, key_weight, value_weight, output_weight, up_weight,
    down_weight, first_gate, second_gate, first_bias, second_bias, first_gain, first_shift,
    second_gain, second_shift,
):
    nbits = nb.bit_length() - 1
    nh = min(3, nbits)
    land_rows = 2 * ROWS + (nbits - nh) * (ROWS >> nh)
    sds = jax.ShapeDtypeStruct
    hbm = pl.BlockSpec(memory_space=pl.ANY)
    vmem = pl.BlockSpec(memory_space=pltpu.VMEM)

    def low(*shape):
        return pltpu.VMEM(shape, BF16)

    def full(*shape):
        return pltpu.VMEM(shape, F32)

    scratch = [
        low(4, LEN, LANE),
        low(LEN, D), low(D, LEN),
        low(D, 768),
        low(D, D), low(D, D), low(D, D),
        low(4, D, D), low(4, D, D),
        full(4, 8, LANE),
        full(4 * OWN, LANE),
        low(4 * OWN, LANE), low(4, OWN, LANE),
        low(LEN, 768),
        low(4, LEN, LEN),
        low(LEN, 2 * LANE), low(OWN, D),
        full(OWN, D), full(OWN, D), full(OWN, D),
        low(OWN, D), low(D, OWN),
        low(4, OWN, D), low(4, OWN, D),
        full(OWN, D),
        low(OWN, D), low(OWN, D),
        full(OWN, D), full(OWN, D),
        low(OWN, D), low(OWN, D),
        low(OWN, D), low(LEN, 2 * LANE),
        full(LANE, LEN), full(LANE, LEN),
        low(LEN, 768),
        full(OWN, D), low(OWN, D), low(OWN, D),
        low(4, OWN, LANE), low(4, OWN, LANE),
        low(4, ROWS, LANE),
        low(2, QKV, LANE), low(land_rows, LANE),
        low(ROWS, LANE),
        full(16, D), full(1 + nbits - nh, 16, LANE),
        full(2 + (1 << nh) + nbits - nh, 16, LANE), full(4, 16, LANE),
        pltpu.SemaphoreType.DMA((224,)),
        pltpu.SemaphoreType.DMA((224,)),
        pltpu.SemaphoreType.DMA((32,)),
    ]
    lo, ig, fin, small = pl.pallas_call(
        functools.partial(layer_kernel, nb),
        out_shape=[
            sds((4 * OWN, LANE), BF16), sds((4 * OWN, LANE), BF16),
            sds((ROWS, LANE), BF16), sds((4, 16, LANE), F32),
        ],
        in_specs=[hbm] * 10 + [vmem] * 6,
        out_specs=[hbm] * 4,
        scratch_shapes=scratch,
        compiler_params=pltpu.CompilerParams(
            collective_id=0, has_side_effects=True, vmem_limit_bytes=63 * 1024 * 1024
        ),
    )(
        tokens, cotangent, query_weight, key_weight, value_weight, output_weight, up_weight,
        down_weight, first_gate, second_gate, first_bias.reshape(1, LANE),
        second_bias.reshape(1, LANE), first_gain.reshape(1, D), first_shift.reshape(1, D),
        second_gain.reshape(1, D), second_shift.reshape(1, D),
    )
    entries = float(nb * 4 * OWN * D)
    outs = pl.pallas_call(
        functools.partial(spread_kernel, entries),
        out_shape=[
            sds((4 * OWN, LANE), BF16), sds((4 * OWN, LANE), F32),
            sds((D, LANE), F32), sds((D, LANE), F32), sds((D, LANE), F32),
            sds((LANE, D), F32), sds((D, D), F32), sds((D, D), F32),
            sds((D, LANE), F32), sds((D, LANE), F32),
            sds((1, LANE), F32), sds((1, LANE), F32),
            sds((1, D), F32), sds((1, D), F32), sds((1, D), F32), sds((1, D), F32),
            sds((1, 4), F32),
        ],
        in_specs=[hbm] * 4,
        out_specs=[hbm] * 17,
        scratch_shapes=[
            low(4 * OWN, LANE), low(4 * OWN, LANE), low(ROWS, LANE), full(4, 16, LANE),
            full(4 * OWN, LANE), full(2, D, D), full(LANE, D), full(5, D, LANE),
            full(2, 1, LANE), full(4, 1, D), full(1, 4),
            pltpu.SemaphoreType.DMA((8,)), pltpu.SemaphoreType.DMA((24,)),
        ],
        compiler_params=pltpu.CompilerParams(vmem_limit_bytes=63 * 1024 * 1024),
    )(lo, ig, fin, small)
    return tuple(outs[:10]) + (
        outs[10].reshape(LANE), outs[11].reshape(LANE), outs[12].reshape(D),
        outs[13].reshape(D), outs[14].reshape(D), outs[15].reshape(D), outs[16].reshape(4),
    )


def solution(mesh):
    cols = P(None, "tensor")
    rows = P("tensor", None)
    both = P("batch", "tensor")
    part = P("tensor")
    in_specs = (
        both, both, cols, cols, cols, rows, cols, rows, cols, cols, part, part, P(), P(), P(), P(),
    )
    out_specs = (
        both, both, cols, cols, cols, rows, cols, rows, cols, cols, part, part,
        P(), P(), P(), P(), P(),
    )
    return jax.shard_map(
        functools.partial(per_device, mesh.shape["batch"]),
        mesh=mesh, in_specs=in_specs, out_specs=out_specs, check_vma=False,
    )
```
